256 devices in a mesh: row: 8 (over y, z_hi), col: 32 (over x, z_lo, core).
Axes of the slice: x: 4, y: 4, z: 8 (z_hi: 2, z_lo: 4; z = z_hi * 4 + z_lo), core: 2. Of those that a mesh axis runs over, the one named last changes fastest.
Arguments:
- inputs: bfloat16 [1024, 12288], P('col', 'row'), may hold values from -1.5 to 1.5
- weight: bfloat16 [12288, 49152], P('row', 'col'), may hold values from -0.21875 to 0.21875
- grad_out: bfloat16 [1024, 49152], P('row', 'col'), may hold values from -0.75 to 0.75
Outputs:
- grad_inputs: bfloat16 [1024, 12288], P('col', 'row')
- grad_weight: bfloat16 [12288, 49152], P('row', 'col')
The draws below stay inside these ranges and needn't reach their ends.
All inputs are finite; a program needn't handle non-finite values.
Results may differ from the reference program's by a relative error of at most 0.0049.
Values may be sent and summed in bfloat16 or wider, within the bound.
A program may use at most 128 MiB of HBM per device.

```python
import math
import jax
import jax.numpy as jnp

D = 12288
FF = 49152
TOKENS = 1024


def block_levels(key, shape, pieces, low, top_value):
    level, own = 1.0, jax.random.fold_in(key, 6)
    for dim, parts in pieces:
        heights = jnp.exp(jax.random.uniform(jax.random.fold_in(own, dim), (parts,), jnp.float32, low / len(pieces), top_value / len(pieces)))
        level = level * jnp.repeat(heights, shape[dim] // parts).reshape([-1 if axis == dim else 1 for axis in range(len(shape))])
    return level


def scatter_about(key, shape, spread, most, cuts=(), held_as=jnp.bfloat16):
    array = spread * jax.random.normal(key, shape, jnp.float32)
    if cuts:
        array = array * block_levels(key, shape, cuts, -0.22, 0.18)
    return jnp.clip(array, -most, most).astype(held_as)


def setup_inputs(seed: int = 0) -> dict:
    seeds = jax.random.split(jax.random.key(seed), 4)
    return {
        "inputs": scatter_about(seeds[0], (TOKENS, D), 0.25, 1.5, ((0, 32), (1, 8))),
        "weight": scatter_about(seeds[1], (D, FF), (D // 16) ** -0.5, 0.21875, ((0, 8), (1, 32))),
        "grad_out": scatter_about(seeds[2], (TOKENS, FF), 0.125, 0.75, ((0, 8), (1, 32))),
    }


def gelu_slope(pre):
    coeff = math.sqrt(2.0 / math.pi)
    inner = coeff * (pre + 0.044715 * pre * pre * pre)
    tanh_val = jnp.tanh(inner)
    return 0.5 * (1.0 + tanh_val) + 0.5 * pre * (1.0 - tanh_val * tanh_val) * coeff * (1.0 + 3.0 * 0.044715 * pre * pre)

def reference(inputs, weight, grad_out):
    pre = jnp.dot(inputs, weight, preferred_element_type=jnp.float32)
    grad_pre = (grad_out.astype(jnp.float32) * gelu_slope(pre)).astype(jnp.bfloat16)
    grad_inputs = jnp.dot(grad_pre, weight.T, preferred_element_type=jnp.float32).astype(jnp.bfloat16)
    grad_weight = jnp.dot(inputs.T, grad_pre, preferred_element_type=jnp.float32).astype(jnp.bfloat16)
    return (grad_inputs, grad_weight)
```

```python
import math

import jax
import jax.numpy as jnp
from jax import lax
from jax.experimental import pallas as pl
from jax.experimental.pallas import tpu as pltpu
from jax.sharding import PartitionSpec as P

MESH = pl.DeviceIdType.MESH
NB = 4
BLK = 16
BF = jnp.bfloat16
F32 = jnp.float32
TILE = 256

OFF = dict(z=0, a=1, c=2, d=3, e=4, f=5, g=6, h=7, i=8, j=9, k=10, l=11, m=12)
NSLOTS = OFF["m"] + NB
GW_FIRST = OFF["j"] + NB - 1


def gelu_slope(pre):
    coeff = math.sqrt(2.0 / math.pi)
    inner = coeff * (pre + 0.044715 * pre * pre * pre)
    tanh_val = jnp.tanh(inner)
    return 0.5 * (1.0 + tanh_val) + 0.5 * pre * (1.0 - tanh_val * tanh_val) * coeff * (
        1.0 + 3.0 * 0.044715 * pre * pre
    )


def kernel(
    inp, w_hbm, go_hbm,
    out, gw_hbm,
    w, go, xs, p32, pb, a_in, bc_in, s_keep, zs, z_in, gp, g32, sib_out, sib_in,
    x_out, x_in, x_keep, t_out, t_in, gwb,
    lsem, wsem, gsem, gwsem,
    zi_s, zi_r, xi_s, xi_r, si_s, si_r, a_s, a_r, b_s, b_r, c_s, c_r, zr_s, zr_r, zg_s, zg_r,
    ga_s, ga_r, gb_s, gb_r, gc_s, gc_r, so_s, so_r, xo_s, xo_r, zo_s, zo_r,
):
    row = lax.axis_index("row")
    col = lax.axis_index("col")
    y, zh = row // 2, row % 2
    x, zl, k = col // 8, (col // 2) % 4, col % 2

    def dev(y=y, zh=zh, x=x, zl=zl, k=k):
        return (y * 2 + zh, (x * 4 + zl) * 2 + k)

    yp, ym = (y + 1) % 4, (y + 3) % 4
    yo = (y + 2) % 4
    d_yp, d_ym = dev(y=yp), dev(y=ym)
    d_zh = dev(zh=1 - zh)
    d_sib = dev(k=1 - k)

    def d_x(d):
        return dev(x=(x + d) % 4)

    def d_z(d):
        return dev(zl=(zl + d) % 4)

    def rc(src, dst, ss, rs, to):
        return pltpu.make_async_remote_copy(
            src_ref=src, dst_ref=dst, send_sem=ss, recv_sem=rs, device_id=to, device_id_type=MESH
        )

    w_cp = pltpu.make_async_copy(w_hbm, w, wsem)
    go_cp = pltpu.make_async_copy(go_hbm, go, gsem)
    w_cp.start()
    go_cp.start()

    barrier = pltpu.get_barrier_semaphore()
    partners = [d_yp, d_ym, d_zh, d_sib] + [d_x(d) for d in (1, 2, 3)] + [d_z(d) for d in (1, 2, 3)]
    for to in partners:
        pl.semaphore_signal(barrier, inc=1, device_id=to, device_id_type=MESH)
    pl.semaphore_wait(barrier, len(partners))

    def gk(g, kk):
        return pl.ds((g * 2 + kk) * 2, 2)

    def zi(b, d):
        return rc(inp.at[b // 2], xs.at[b, (x * 2 + k) * 2 + zl // 2], zi_s.at[b, d - 1], zi_r.at[b, zl // 2], d_z(d))

    def zi_wait(b, h):
        r = xs.at[b, (x * 2 + k) * 2 + h]
        return rc(r, r, zi_s.at[b, 0], zi_r.at[b, h], d_z(1))

    def own_copy(b):
        return pltpu.make_async_copy(inp.at[b // 2], xs.at[b, (x * 2 + k) * 2 + zl // 2], lsem.at[b])

    def xi(b, d):
        r = xs.at[b, gk(x, k)]
        return rc(r, r, xi_s.at[b, d - 1], xi_r.at[b, d - 1], d_x(d))

    def si(b, d):
        r = xs.at[b, gk((x + d) % 4, k)]
        return rc(r, r, si_s.at[b, d], si_r.at[b, d], d_sib)

    def a_cp(b, n):
        return rc(pb.at[b, gk(yo, n)], a_in.at[b, n], a_s.at[b, n], a_r.at[b, n], (d_yp, d_ym)[n])

    def b_cp(b, n):
        return rc(
            pb.at[b, gk((yp, ym)[n], 1 - n)], bc_in.at[b, n, 1 - n], b_s.at[b, n], b_r.at[b, n], (d_yp, d_ym)[n]
        )

    def c_cp(b, n):
        return rc(pb.at[b, gk((yp, ym)[n], n)], bc_in.at[b, n, n], c_s.at[b, n], c_r.at[b, n], (d_yp, d_ym)[n])

    def zr(b):
        return rc(zs.at[b], z_in.at[b], zr_s.at[b], zr_r.at[b], d_zh)

    def zg(b, kk):
        r = gp.at[b, (y * 2 + kk) * 2 + zh]
        return rc(r, r, zg_s.at[b, kk], zg_r.at[b, kk], d_zh)

    def ga(b, n):
        r = gp.at[b, gk(y, n)]
        return rc(r, r, ga_s.at[b, n], ga_r.at[b, n], (d_yp, d_ym)[n])

    def gb(b, n):
        r = gp.at[b, gk(y, 1 - n)]
        return rc(r, r, gb_s.at[b, n], gb_r.at[b, n], (d_yp, d_ym)[n])

    def gc(b, n):
        r = gp.at[b, gk((ym, yp)[n], n)]
        return rc(r, r, gc_s.at[b, n], gc_r.at[b, n], (d_yp, d_ym)[n])

    def so(b):
        return rc(sib_out.at[b], sib_in.at[b], so_s.at[b], so_r.at[b], d_sib)

    def xo(b, d):
        return rc(x_out.at[b, d - 1], x_in.at[b, d - 1], xo_s.at[b, d - 1], xo_r.at[b, d - 1], d_x(d))

    def zo(b, d):
        return rc(t_out.at[b, d - 1], t_in.at[b, d - 1], zo_s.at[b, d - 1], zo_r.at[b, d - 1], d_z(d))

    def st_z(b):
        @pl.when(zl % 2 == b % 2)
        def _():
            for d in (1, 2, 3):
                zi(b, d).start()
            own_copy(b).start()

    def st_a(b):
        for h in range(2):
            @pl.when(zl != 2 * h + b % 2)
            def _():
                zi_wait(b, h).wait_recv()

            @pl.when(zl == 2 * h + b % 2)
            def _():
                own_copy(b).wait()
        for d in (1, 3, 2):
            xi(b, d).start()
        si(b, 0).start()

    def st_c(b):
        for d in (1, 3, 2):
            xi(b, d).wait_recv()
            si(b, 4 - d).start()

    def st_d(b):
        for d in range(4):
            si(b, d).wait_recv()

        @pl.when(b == 0)
        def _():
            w_cp.wait()

        @pl.loop(0, 1536 // TILE)
        def _(t):
            cols = pl.ds(pl.multiple_of(t * TILE, TILE), TILE)
            acc = jnp.dot(xs[b].reshape(256, 1536), w[:, cols], preferred_element_type=F32).reshape(16, BLK, TILE)
            p32[b, :, :, cols] = acc
            pb[b, :, :, cols] = acc.astype(BF)

        for n in range(2):
            a_cp(b, n).start()
        for n in range(2):
            b_cp(b, n).start()

    def st_e(b):
        for n in range(2):
            a_cp(b, n).wait_recv()
            r = gk((yp, ym)[n], n)
            pb[b, r] = (p32[b, r] + a_in[b, n].astype(F32)).astype(BF)
            c_cp(b, n).start()

    def st_f(b):
        for n in range(2):
            b_cp(b, n).wait_recv()
        for n in range(2):
            c_cp(b, n).wait_recv()
        for kk in range(2):
            def total(h):
                return (
                    p32[b, (y * 2 + kk) * 2 + h]
                    + bc_in[b, 0, kk, h].astype(F32)
                    + bc_in[b, 1, kk, h].astype(F32)
                )
            s_keep[b, kk] = total(zh)
            zs[b, kk] = total(1 - zh).astype(BF)
        zr(b).start()

    def st_g(b):
        @pl.when(b == 0)
        def _():
            go_cp.wait()

        zr(b).wait_recv()
        for kk in range(2):
            pre = s_keep[b, kk] + z_in[b, kk].astype(F32)
            gp[b, (y * 2 + kk) * 2 + zh] = (go[b % 2, kk, b // 2].astype(F32) * gelu_slope(pre)).astype(BF)
            zg(b, kk).start()

    def st_h(b):
        for kk in range(2):
            r = gp.at[b, (y * 2 + kk) * 2 + 1 - zh]
            rc(r, r, zg_s.at[b, kk], zg_r.at[b, kk], d_zh).wait_recv()
        for n in range(2):
            ga(b, n).start()
        for n in range(2):
            gb(b, n).start()

    def st_i(b):
        for n in range(2):
            r = gp.at[b, gk((ym, yp)[n], n)]
            rc(r, r, ga_s.at[b, n], ga_r.at[b, n], (d_yp, d_ym)[n]).wait_recv()
            gc(b, n).start()

    def st_j(b):
        for n in range(2):
            r = gp.at[b, gk((ym, yp)[n], 1 - n)]
            rc(r, r, gb_s.at[b, n], gb_r.at[b, n], (d_yp, d_ym)[n]).wait_recv()
        for n in range(2):
            r = gp.at[b, gk(yo, n)]
            rc(r, r, gc_s.at[b, n], gc_r.at[b, n], (d_yp, d_ym)[n]).wait_recv()

        @pl.loop(0, 1536 // TILE)
        def _(t):
            o = pl.multiple_of(t * TILE, TILE)
            acc = lax.dot_general(
                gp[b].reshape(256, 1536), w[pl.ds(o, TILE), :], (((1,), (1,)), ((), ())), preferred_element_type=F32
            )
            g32[b, :, :, pl.ds(o, TILE)] = acc.reshape(16, BLK, TILE)

        for g in range(4):
            sib_out[b, pl.ds(2 * g, 2)] = g32[b, gk(g, 1 - k)].astype(BF)
        so(b).start()

    def st_k(b):
        so(b).wait_recv()

        def total(g):
            return g32[b, gk(g, k)] + sib_in[b, pl.ds(2 * g, 2)].astype(F32)

        for d in (1, 3, 2):
            x_out[b, d - 1] = total((x + d) % 4).astype(BF)
            xo(b, d).start()
        x_keep[b] = total(x)

    def st_l(b):
        for d in (1, 3, 2):
            xo(b, d).wait_recv()
        for h in range(2):
            tot = x_keep[b, h]
            for d in range(3):
                tot = tot + x_in[b, d, h].astype(F32)
            x_keep[b, h] = tot
            to = 2 * h + b % 2
            for d in (1, 2, 3):
                @pl.when((zl + d) % 4 == to)
                def _():
                    t_out[b, d - 1] = x_keep[b, h].astype(BF)
                    zo(b, d).start()

    def st_m(b):
        @pl.when(zl % 2 == b % 2)
        def _():
            tot = x_keep[b, zl // 2]
            for d in (1, 2, 3):
                zo(b, d).wait_recv()
            for d in range(3):
                tot = tot + t_in[b, d].astype(F32)
            out[b // 2] = tot.astype(BF)

    def gw_out(t):
        rows = pl.ds(t * TILE if isinstance(t, int) else pl.multiple_of(t * TILE, TILE), TILE)
        return pltpu.make_async_copy(gwb.at[rows], gw_hbm.at[rows], gwsem.at[t])

    def gw_tile(t):
        o = pl.multiple_of(t * TILE, TILE)
        acc = lax.dot_general(
            xs[:, :, :, pl.ds(o, TILE)].reshape(1024, TILE),
            gp[...].reshape(1024, 1536),
            (((0,), (0,)), ((), ())),
            preferred_element_type=F32,
        )
        gwb[pl.ds(o, TILE), :] = acc.astype(BF)
        gw_out(t).start()

    stages = dict(z=st_z, a=st_a, c=st_c, d=st_d, e=st_e, f=st_f, g=st_g, h=st_h, i=st_i, j=st_j, k=st_k, l=st_l, m=st_m)

    @pl.loop(0, NSLOTS)
    def _(slot):
        for name in "mlkjihgfedcaz":
            b = slot - OFF[name]

            @pl.when((b >= 0) & (b < NB))
            def _():
                stages[name](b)

        @pl.when((slot >= GW_FIRST) & (slot < GW_FIRST + 3))
        def _():
            @pl.loop(0, 2)
            def _(t):
                gw_tile((slot - GW_FIRST) * 2 + t)

    @pl.loop(0, NB)
    def _(b):
        @pl.when(zl % 2 == b % 2)
        def _():
            for d in (1, 2, 3):
                zi(b, d).wait_send()
        for d in (1, 2, 3):
            xi(b, d).wait_send()
            xo(b, d).wait_send()

            @pl.when((zl + d) % 2 == b % 2)
            def _():
                zo(b, d).wait_send()
        for d in range(4):
            si(b, d).wait_send()
        for n in range(2):
            for cp in (a_cp, b_cp, c_cp, zg, ga, gb, gc):
                cp(b, n).wait_send()
        zr(b).wait_send()
        so(b).wait_send()

    for t in range(6):
        gw_out(t).wait()


def per_device(inputs, weight, grad_out):
    any_ = pl.BlockSpec(memory_space=pl.ANY)
    vmem = pl.BlockSpec(memory_space=pltpu.VMEM)
    V = pltpu.VMEM
    D = pltpu.SemaphoreType.DMA
    sems = []
    for shape in (
        (NB, 3), (NB, 2),
        (NB, 3), (NB, 3),
        (NB, 4), (NB, 4),
        (NB, 2), (NB, 2), (NB, 2), (NB, 2), (NB, 2), (NB, 2),
        (NB,), (NB,),
        (NB, 2), (NB, 2),
        (NB, 2), (NB, 2), (NB, 2), (NB, 2), (NB, 2), (NB, 2),
        (NB,), (NB,),
        (NB, 3), (NB, 3),
        (NB, 3), (NB, 3),
    ):
        sems.append(D(shape))
    grad_inputs, grad_weight = pl.pallas_call(
        kernel,
        out_shape=(
            jax.ShapeDtypeStruct((2, BLK, 1536), BF),
            jax.ShapeDtypeStruct((1536, 1536), BF),
        ),
        in_specs=[vmem, any_, any_],
        out_specs=(vmem, any_),
        scratch_shapes=[
            V((1536, 1536), BF),
            V((2, 2, 2, BLK, 1536), BF),
            V((NB, 16, BLK, 1536), BF),
            V((NB, 16, BLK, 1536), F32),
            V((NB, 16, BLK, 1536), BF),
            V((NB, 2, 2, BLK, 1536), BF),
            V((NB, 2, 2, 2, BLK, 1536), BF),
            V((NB, 2, BLK, 1536), F32),
            V((NB, 2, BLK, 1536), BF),
            V((NB, 2, BLK, 1536), BF),
            V((NB, 16, BLK, 1536), BF),
            V((NB, 16, BLK, 1536), F32),
            V((NB, 8, BLK, 1536), BF),
            V((NB, 8, BLK, 1536), BF),
            V((NB, 3, 2, BLK, 1536), BF),
            V((NB, 3, 2, BLK, 1536), BF),
            V((NB, 2, BLK, 1536), F32),
            V((NB, 3, BLK, 1536), BF),
            V((NB, 3, BLK, 1536), BF),
            V((1536, 1536), BF),
            D((NB,)), D, D, D((6,)),
            *sems,
        ],
        compiler_params=pltpu.CompilerParams(
            collective_id=0, has_side_effects=True, vmem_limit_bytes=60 * 2**20
        ),
        cost_estimate=pl.CostEstimate(flops=3 * 2 * 1024 * 1536 * 1536, bytes_accessed=10**7, transcendentals=128 * 1536),
    )(inputs.reshape(2, BLK, 1536), weight, grad_out.reshape(2, 2, 2, BLK, 1536))
    return grad_inputs.reshape(32, 1536), grad_weight


def solution(mesh):
    return jax.shard_map(
        per_device,
        mesh=mesh,
        in_specs=(P("col", "row"), P("row", "col"), P("row", "col")),
        out_specs=(P("col", "row"), P("row", "col")),
        check_vma=False,
    )
```

```python
import math

import jax
import jax.numpy as jnp
from jax import lax
from jax.experimental import pallas as pl
from jax.experimental.pallas import tpu as pltpu
from jax.sharding import PartitionSpec as P

MESH = pl.DeviceIdType.MESH
NB = 4
BLK = 16
BF = jnp.bfloat16
F32 = jnp.float32
TILE = 256

PIECES = 8
HALF = 768
NS = 2 * NB

ORDER = (('h', 13), ('e', 8), ('l', 21), ('j', 17), ('g', 11), ('k', 18), ('m', 37), ('i', 14), ('f', 9), ('d', 6), ('a', 2), ('c', 5), ('z', 0))
DRY = {'d': 5, 'j': 6}
NSLOTS = max(first for _, first in ORDER) + NS
GW_FIRST = dict(ORDER)["j"] + NS - 1
GW_EACH = 2


def gelu_slope(pre):
    coeff = math.sqrt(2.0 / math.pi)
    inner = coeff * (pre + 0.044715 * pre * pre * pre)
    tanh_val = jnp.tanh(inner)
    return 0.5 * (1.0 + tanh_val) + 0.5 * pre * (1.0 - tanh_val * tanh_val) * coeff * (
        1.0 + 3.0 * 0.044715 * pre * pre
    )


def kernel(
    inp, w_hbm, go_hbm,
    out, gw_hbm,
    w, go, xs, p32, pb, a_in, bc_in, s_keep, zs, z_in, gp, g32, sib_out, sib_in,
    x_out, x_in, x_keep, t_out, t_in, gwb,
    lsem, wsem, gsem, gwsem,
    zi_s, zi_r, xi_s, xi_r, si_s, si_r, abc_s, a_r, bc_r, zr_s, zr_r, zg_s, zg_r, g_s, ga_r, gbc_r,
    so_s, so_r, xo_s, xo_r, zo_s, zo_r,
):
    row = lax.axis_index("row")
    col = lax.axis_index("col")
    y, zh = row // 2, row % 2
    x, zl, k = col // 8, (col // 2) % 4, col % 2

    def dev(y=y, zh=zh, x=x, zl=zl, k=k):
        return (y * 2 + zh, (x * 4 + zl) * 2 + k)

    yp, ym = (y + 1) % 4, (y + 3) % 4
    yo = (y + 2) % 4
    d_yp, d_ym = dev(y=yp), dev(y=ym)
    d_zh = dev(zh=1 - zh)
    d_sib = dev(k=1 - k)

    def d_x(d):
        return dev(x=(x + d) % 4)

    def d_z(d):
        return dev(zl=(zl + d) % 4)

    def rc(src, dst, ss, rs, to):
        return pltpu.make_async_remote_copy(
            src_ref=src, dst_ref=dst, send_sem=ss, recv_sem=rs, device_id=to, device_id_type=MESH
        )

    w_cp = pltpu.make_async_copy(w_hbm, w, wsem)
    go_cp = pltpu.make_async_copy(go_hbm, go, gsem)
    w_cp.start()
    go_cp.start()

    barrier = pltpu.get_barrier_semaphore()
    partners = [d_yp, d_ym, d_zh, d_sib] + [d_x(d) for d in (1, 2, 3)] + [d_z(d) for d in (1, 2, 3)]
    for to in partners:
        pl.semaphore_signal(barrier, inc=1, device_id=to, device_id_type=MESH)
    pl.semaphore_wait(barrier, len(partners))

    def gk(g, kk):
        return pl.ds((g * 2 + kk) * 2, 2)

    def sent(region, sem):
        rc(region, region, sem, so_r.at[0], d_sib).wait_send()

    def arrived(region, sem):
        rc(region, region, so_s, sem, d_sib).wait_recv()

    def part(b):
        return ((b + 1) // 2) % 2

    def source(b, h):
        return (2 + part(b)) if h else (1 - part(b))

    def mine(b):
        return ((zl + 1) // 2) % 2 != part(b)

    def zi(b, d):
        return rc(inp.at[b // 2], xs.at[b, x, k, zl // 2], zi_s.at[b], zi_r.at[b, zl // 2], d_z(d))

    def own_copy(b):
        return pltpu.make_async_copy(inp.at[b // 2], xs.at[b, x, k, zl // 2], lsem.at[b])

    def xi(b, d):
        r = xs.at[b, x, k]
        return rc(r, r, xi_s, xi_r.at[b], d_x(d))

    def si(b):
        r = xs.at[b, :, k]
        return rc(r, r, si_s, si_r.at[b], d_sib)

    def a_cp(n, i):
        return rc(pb.at[n, gk(yo, i)], a_in.at[n, i], abc_s, a_r.at[n, i], (d_yp, d_ym)[i])

    def b_cp(n, i):
        return rc(pb.at[n, gk((yp, ym)[i], 1 - i)], bc_in.at[n, i, 1 - i], abc_s, bc_r.at[n], (d_yp, d_ym)[i])

    def c_cp(n, i):
        return rc(pb.at[n, gk((yp, ym)[i], i)], bc_in.at[n, i, i], abc_s, bc_r.at[n], (d_yp, d_ym)[i])

    def zr(n):
        return rc(zs.at[n], z_in.at[n], zr_s, zr_r.at[n], d_zh)

    def zg(n):
        r = gp.at[n, y, :, zh]
        return rc(r, r, zg_s, zg_r.at[n], d_zh)

    def ga(n, i):
        r = gp.at[n, y, i]
        return rc(r, r, g_s, ga_r.at[n, i], (d_yp, d_ym)[i])

    def gb(n, i):
        r = gp.at[n, y, 1 - i]
        return rc(r, r, g_s, gbc_r.at[n // 2], (d_yp, d_ym)[i])

    def gc(n, i):
        r = gp.at[n, (ym, yp)[i], i]
        return rc(r, r, g_s, gbc_r.at[n // 2], (d_yp, d_ym)[i])

    def so(n):
        return rc(sib_out.at[n], sib_in.at[n], so_s, so_r.at[n], d_sib)

    def xo(n, d):
        return rc(x_out.at[n, d - 1], x_in.at[n, d - 1], xo_s, xo_r.at[n], d_x(d))

    def zo(n, d):
        return rc(t_out.at[n, d - 1], t_in.at[n, d - 1], zo_s.at[n], zo_r.at[n], d_z(d))

    def half(q, t=0, size=HALF):
        return pl.ds(pl.multiple_of(q * HALF + t * size, size), size)

    def st_z(b):
        @pl.when(mine(b))
        def _():
            for d in (1, 2, 3):
                zi(b, d).start()
            own_copy(b).start()

    def st_a(b):
        for h in range(2):
            @pl.when(zl != source(b, h))
            def _():
                arrived(xs.at[b, x, k, h], zi_r.at[b, h])

            @pl.when(zl == source(b, h))
            def _():
                own_copy(b).wait()
        for d in (1, 3, 2):
            xi(b, d).start()

    def st_c(b):
        arrived(xs.at[b, pl.ds(0, 3), k], xi_r.at[b])
        si(b).start()

    def st_d(n):
        b, q = n // 2, n % 2

        @pl.when((q == 0) & (n < NS))
        def _():
            arrived(xs.at[b, :, 1 - k], si_r.at[b])

        @pl.when(n == NS)
        def _():
            w_cp.wait()

        @pl.loop(0, jnp.where(n < NS, HALF // TILE, 1))
        def _(t):
            cols = pl.ds(pl.multiple_of(t * TILE, TILE), TILE)
            acc = jnp.dot(xs[b].reshape(256, 1536), w[:, half(q, t, TILE)], preferred_element_type=F32)
            acc = acc.reshape(16, BLK, TILE)
            p32[n, :, :, cols] = acc
            pb[n, :, :, cols] = acc.astype(BF)

        @pl.when(n < NS)
        def _():
            for i in range(2):
                a_cp(n, i).start()
            for i in range(2):
                b_cp(n, i).start()

    def st_e(n):
        for i in range(2):
            arrived(a_in.at[n, i], a_r.at[n, i])
            r = gk((yp, ym)[i], i)
            pb[n, r] = (p32[n, r] + a_in[n, i].astype(F32)).astype(BF)
            c_cp(n, i).start()

    def st_f(n):
        arrived(bc_in.at[n], bc_r.at[n])
        for kk in range(2):
            def total(h):
                return (
                    p32[n, (y * 2 + kk) * 2 + h]
                    + bc_in[n, 0, kk, h].astype(F32)
                    + bc_in[n, 1, kk, h].astype(F32)
                )
            s_keep[n, kk] = total(zh)
            zs[n, kk] = total(1 - zh).astype(BF)
        zr(n).start()

    def st_g(n):
        b, q = n // 2, n % 2

        @pl.when(n == 0)
        def _():
            go_cp.wait()

        arrived(z_in.at[n], zr_r.at[n])
        line = part(b) * zh + (1 - part(b)) * (1 - zh)
        for kk in range(2):
            pre = s_keep[n, kk] + z_in[n, kk].astype(F32)
            cot = go[line, kk, b // 2, :, half(q)].astype(F32)
            gp[n, y, kk, zh] = (cot * gelu_slope(pre)).astype(BF)
        zg(n).start()

    def st_h(n):
        arrived(gp.at[n, y, :, 1 - zh], zg_r.at[n])
        for i in range(2):
            ga(n, i).start()
        for i in range(2):
            gb(n, i).start()

    def st_i(n):
        for i in range(2):
            arrived(gp.at[n, (ym, yp)[i], i], ga_r.at[n, i])
            gc(n, i).start()

    def st_j(n):
        b, q = n // 2, n % 2

        @pl.when((q == 0) & (n < NS))
        def _():
            arrived(gp.at[pl.ds(2 * b, 2), pl.ds(0, 2)], gbc_r.at[b])

        @pl.loop(0, jnp.where(n < NS, HALF // TILE, 1))
        def _(t):
            rows = half(q, t, TILE)
            acc = 0.0
            for p in range(2):
                acc += lax.dot_general(
                    gp[2 * b + p].reshape(256, HALF),
                    w[rows, p * HALF : (p + 1) * HALF],
                    (((1,), (1,)), ((), ())),
                    preferred_element_type=F32,
                )
            g32[n, :, :, pl.ds(pl.multiple_of(t * TILE, TILE), TILE)] = acc.reshape(16, BLK, TILE)

        @pl.when(n < NS)
        def _():
            for g in range(4):
                sib_out[n, pl.ds(2 * g, 2)] = g32[n, gk(g, 1 - k)].astype(BF)
            so(n).start()

    def st_k(n):
        arrived(sib_in.at[n], so_r.at[n])

        def total(g):
            return g32[n, gk(g, k)] + sib_in[n, pl.ds(2 * g, 2)].astype(F32)

        for d in (1, 3, 2):
            x_out[n, d - 1] = total((x + d) % 4).astype(BF)
            xo(n, d).start()
        x_keep[n] = total(x)

    def st_l(n):
        b = n // 2
        arrived(x_in.at[n], xo_r.at[n])
        for h in range(2):
            tot = x_keep[n, h]
            for d in range(3):
                tot = tot + x_in[n, d, h].astype(F32)
            x_keep[n, h] = tot
            to = source(b, h)
            for d in (1, 2, 3):
                @pl.when((zl + d) % 4 == to)
                def _():
                    t_out[n, d - 1] = x_keep[n, h].astype(BF)
                    zo(n, d).start()

    def st_m(n):
        b, q = n // 2, n % 2

        @pl.when(mine(b))
        def _():
            tot = x_keep[n, zl // 2]
            arrived(t_in.at[n], zo_r.at[n])
            for d in range(3):
                tot = tot + t_in[n, d].astype(F32)
            out[b // 2, :, half(q)] = tot.astype(BF)

    def gw_out(t):
        rows = pl.ds(t * TILE if isinstance(t, int) else pl.multiple_of(t * TILE, TILE), TILE)
        return pltpu.make_async_copy(gwb.at[rows], gw_hbm.at[rows], gwsem.at[t])

    def gw_tile(t):
        o = pl.multiple_of(t * TILE, TILE)
        lhs = xs[:NB, :, :, :, :, pl.ds(o, TILE)].reshape(1024, TILE)
        for p in range(2):
            rhs = jnp.concatenate([gp[2 * b + p].reshape(256, HALF) for b in range(NB)], axis=0)
            acc = lax.dot_general(lhs, rhs, (((0,), (0,)), ((), ())), preferred_element_type=F32)
            gwb[pl.ds(o, TILE), p * HALF : (p + 1) * HALF] = acc.astype(BF)
        gw_out(t).start()

    stages = dict(z=st_z, a=st_a, c=st_c, d=st_d, e=st_e, f=st_f, g=st_g, h=st_h, i=st_i, j=st_j, k=st_k, l=st_l, m=st_m)

    xs[NB] = jnp.zeros((4, 2, 2, BLK, 1536), BF)
    gp[NS] = jnp.zeros((4, 2, 2, BLK, HALF), BF)
    gp[NS + 1] = jnp.zeros((4, 2, 2, BLK, HALF), BF)

    @pl.loop(0, NSLOTS)
    def _(slot):
        for name, first in ORDER:
            n = slot - first
            go_now = (n >= 0) & (n < NS)
            if name in DRY:
                go_now = go_now | (slot == DRY[name])
                n = jnp.where(slot == DRY[name], NS, n)
            if name in "zac":
                go_now = go_now & (n % 2 == 0)
                n = n // 2

            @pl.when(go_now)
            def _():
                stages[name](n)

        @pl.when((slot >= GW_FIRST) & (slot < GW_FIRST + 6 // GW_EACH))
        def _():
            @pl.loop(0, GW_EACH)
            def _(t):
                gw_tile((slot - GW_FIRST) * GW_EACH + t)

    for b in range(NB):
        @pl.when(mine(b))
        def _():
            sent(xs.at[b, pl.ds(0, 3), 0, 0], zi_s.at[b])

    for n in range(NS):
        @pl.when(mine(n // 2))
        def _():
            sent(t_out.at[n, 0], zo_s.at[n])

        @pl.when(jnp.logical_not(mine(n // 2)))
        def _():
            sent(t_out.at[n, pl.ds(0, 2)], zo_s.at[n])

    sent(xs.at[pl.ds(0, NB), pl.ds(0, 3), 0], xi_s)
    sent(xs.at[pl.ds(0, NB), :, 0], si_s)
    sent(pb.at[pl.ds(0, NS), pl.ds(0, 12)], abc_s)
    sent(zs, zr_s)
    sent(gp.at[pl.ds(0, NS), 0, 0], zg_s)
    sent(gp.at[pl.ds(0, NS), pl.ds(0, 3)], g_s)
    sent(sib_out, so_s)
    sent(x_out, xo_s)

    for t in range(6):
        gw_out(t).wait()


def place(gi, gw, gi_out, gw_out, gi_buf, gw_buf, in_sem, out_sem):
    size = 1536 // PIECES
    ways = []
    for p in range(PIECES):
        rows = pl.ds(p * size, size)
        ways.append((gw.at[rows], gw_buf.at[rows], gw_out.at[rows]))
    ways.append((gi, gi_buf, gi_out))
    into = [pltpu.make_async_copy(src, buf, in_sem.at[p]) for p, (src, buf, _) in enumerate(ways)]
    onto = [pltpu.make_async_copy(buf, dst, out_sem.at[p]) for p, (_, buf, dst) in enumerate(ways)]
    for copy in into:
        copy.start()
    for first, second in zip(into, onto):
        first.wait()
        second.start()
    for copy in onto:
        copy.wait()


def per_device(inputs, weight, grad_out):
    any_ = pl.BlockSpec(memory_space=pl.ANY)
    vmem = pl.BlockSpec(memory_space=pltpu.VMEM)
    V = pltpu.VMEM
    D = pltpu.SemaphoreType.DMA
    sems = [
        D((NB,)), D((NB, 2)),
        D, D((NB,)),
        D, D((NB,)),
        D, D((NS, 2)), D((NS,)),
        D, D((NS,)),
        D, D((NS,)),
        D, D((NS, 2)), D((NB,)),
        D, D((NS,)),
        D, D((NS,)),
        D((NS,)), D((NS,)),
    ]
    grad_inputs, grad_weight = pl.pallas_call(
        kernel,
        out_shape=(
            jax.ShapeDtypeStruct((2, BLK, 1536), BF),
            jax.ShapeDtypeStruct((1536, 1536), BF),
        ),
        in_specs=[vmem, any_, any_],
        out_specs=(vmem, any_),
        scratch_shapes=[
            V((1536, 1536), BF),
            V((2, 2, 2, BLK, 1536), BF),
            V((NB + 1, 4, 2, 2, BLK, 1536), BF),
            V((NS + 1, 16, BLK, HALF), F32),
            V((NS + 1, 16, BLK, HALF), BF),
            V((NS, 2, 2, BLK, HALF), BF),
            V((NS, 2, 2, 2, BLK, HALF), BF),
            V((NS, 2, BLK, HALF), F32),
            V((NS, 2, BLK, HALF), BF),
            V((NS, 2, BLK, HALF), BF),
            V((NS + 2, 4, 2, 2, BLK, HALF), BF),
            V((NS + 1, 16, BLK, HALF), F32),
            V((NS, 8, BLK, HALF), BF),
            V((NS, 8, BLK, HALF), BF),
            V((NS, 3, 2, BLK, HALF), BF),
            V((NS, 3, 2, BLK, HALF), BF),
            V((NS, 2, BLK, HALF), F32),
            V((NS, 3, BLK, HALF), BF),
            V((NS, 3, BLK, HALF), BF),
            V((1536, 1536), BF),
            D((NB,)), D, D, D((6,)),
            *sems,
        ],
        compiler_params=pltpu.CompilerParams(
            collective_id=0, has_side_effects=True, vmem_limit_bytes=60 * 2**20
        ),
        cost_estimate=pl.CostEstimate(flops=3 * 2 * 1024 * 1536 * 1536, bytes_accessed=10**7, transcendentals=128 * 1536),
    )(inputs.reshape(2, BLK, 1536), weight, grad_out.reshape(2, 2, 2, BLK, 1536))
    grad_inputs, grad_weight = pl.pallas_call(
        place,
        out_shape=(jax.ShapeDtypeStruct((2, BLK, 1536), BF), jax.ShapeDtypeStruct((1536, 1536), BF)),
        in_specs=[any_, any_],
        out_specs=(any_, any_),
        scratch_shapes=[V((2, BLK, 1536), BF), V((1536, 1536), BF), D((PIECES + 1,)), D((PIECES + 1,))],
        compiler_params=pltpu.CompilerParams(vmem_limit_bytes=60 * 2**20),
    )(grad_inputs, grad_weight)
    return grad_inputs.reshape(32, 1536), grad_weight


def solution(mesh):
    return jax.shard_map(
        per_device,
        mesh=mesh,
        in_specs=(P("col", "row"), P("row", "col"), P("row", "col")),
        out_specs=(P("col", "row"), P("row", "col")),
        check_vma=False,
    )
```

```python
import math

import jax
import jax.numpy as jnp
from jax import lax
from jax.experimental import pallas as pl
from jax.experimental.pallas import tpu as pltpu
from jax.sharding import PartitionSpec as P

MESH = pl.DeviceIdType.MESH
NB = 4
BLK = 16
BF = jnp.bfloat16
F32 = jnp.float32
TILE = 256

PIECES = 8
HALF = 768
NS = 2 * NB

ORDER = (('h', 13), ('e', 8), ('l', 21), ('j', 17), ('g', 11), ('k', 18), ('m', 29), ('i', 14), ('f', 9), ('d', 6), ('a', 2), ('c', 5), ('z', 0))
NSLOTS = max(first for _, first in ORDER) + NS
GW_FIRST = dict(ORDER)["j"] + NS - 1
GW_EACH = 2


def gelu_slope(pre):
    coeff = math.sqrt(2.0 / math.pi)
    inner = coeff * (pre + 0.044715 * pre * pre * pre)
    tanh_val = jnp.tanh(inner)
    return 0.5 * (1.0 + tanh_val) + 0.5 * pre * (1.0 - tanh_val * tanh_val) * coeff * (
        1.0 + 3.0 * 0.044715 * pre * pre
    )


def kernel(
    inp, w_hbm, go_hbm,
    out, gw_hbm,
    w, go, xs, p32, pb, a_in, bc_in, s_keep, zs, z_in, gp, g32, sib_out, sib_in,
    x_out, x_in, x_keep, t_out, t_in, gwb,
    lsem, wsem, gsem, gwsem,
    zi_s, zi_r, xi_s, xi_r, si_s, si_r, abc_s, a_r, bc_r, zr_s, zr_r, zg_s, zg_r, g_s, ga_r, gbc_r,
    so_s, so_r, xo_s, xo_r, zo_s, zo_r,
):
    row = lax.axis_index("row")
    col = lax.axis_index("col")
    y, zh = row // 2, row % 2
    x, zl, k = col // 8, (col // 2) % 4, col % 2

    def dev(y=y, zh=zh, x=x, zl=zl, k=k):
        return (y * 2 + zh, (x * 4 + zl) * 2 + k)

    yp, ym = (y + 1) % 4, (y + 3) % 4
    yo = (y + 2) % 4
    d_yp, d_ym = dev(y=yp), dev(y=ym)
    d_zh = dev(zh=1 - zh)
    d_sib = dev(k=1 - k)

    def d_x(d):
        return dev(x=(x + d) % 4)

    def d_z(d):
        return dev(zl=(zl + d) % 4)

    def rc(src, dst, ss, rs, to):
        return pltpu.make_async_remote_copy(
            src_ref=src, dst_ref=dst, send_sem=ss, recv_sem=rs, device_id=to, device_id_type=MESH
        )

    w_cp = pltpu.make_async_copy(w_hbm, w, wsem)
    go_cp = pltpu.make_async_copy(go_hbm, go, gsem)
    w_cp.start()
    go_cp.start()

    barrier = pltpu.get_barrier_semaphore()
    partners = [d_yp, d_ym, d_zh, d_sib] + [d_x(d) for d in (1, 2, 3)] + [d_z(d) for d in (1, 2, 3)]
    for to in partners:
        pl.semaphore_signal(barrier, inc=1, device_id=to, device_id_type=MESH)
    pl.semaphore_wait(barrier, len(partners))

    def gk(g, kk):
        return pl.ds((g * 2 + kk) * 2, 2)

    def sent(region, sem):
        rc(region, region, sem, so_r.at[0], d_sib).wait_send()

    def arrived(region, sem):
        rc(region, region, so_s, sem, d_sib).wait_recv()

    def part(b):
        return ((b + 1) // 2) % 2

    def source(b, h):
        return (2 + part(b)) if h else (1 - part(b))

    def mine(b):
        return ((zl + 1) // 2) % 2 != part(b)

    def zi(b, d):
        return rc(inp.at[b // 2], xs.at[b, x, k, zl // 2], zi_s.at[b], zi_r.at[b, zl // 2], d_z(d))

    def own_copy(b):
        return pltpu.make_async_copy(inp.at[b // 2], xs.at[b, x, k, zl // 2], lsem.at[b])

    def xi(b, d):
        r = xs.at[b, x, k]
        return rc(r, r, xi_s, xi_r.at[b], d_x(d))

    def si(b):
        r = xs.at[b, :, k]
        return rc(r, r, si_s, si_r.at[b], d_sib)

    def a_cp(n, i):
        return rc(pb.at[n, gk(yo, i)], a_in.at[n, i], abc_s, a_r.at[n, i], (d_yp, d_ym)[i])

    def b_cp(n, i):
        return rc(pb.at[n, gk((yp, ym)[i], 1 - i)], bc_in.at[n, i, 1 - i], abc_s, bc_r.at[n], (d_yp, d_ym)[i])

    def c_cp(n, i):
        return rc(pb.at[n, gk((yp, ym)[i], i)], bc_in.at[n, i, i], abc_s, bc_r.at[n], (d_yp, d_ym)[i])

    def zr(n):
        return rc(zs.at[n], z_in.at[n], zr_s, zr_r.at[n], d_zh)

    def zg(n):
        r = gp.at[n, y, :, zh]
        return rc(r, r, zg_s, zg_r.at[n], d_zh)

    def ga(n, i):
        r = gp.at[n, y, i]
        return rc(r, r, g_s, ga_r.at[n, i], (d_yp, d_ym)[i])

    def gb(n, i):
        r = gp.at[n, y, 1 - i]
        return rc(r, r, g_s, gbc_r.at[n // 2], (d_yp, d_ym)[i])

    def gc(n, i):
        r = gp.at[n, (ym, yp)[i], i]
        return rc(r, r, g_s, gbc_r.at[n // 2], (d_yp, d_ym)[i])

    def so(n):
        return rc(sib_out.at[n], sib_in.at[n], so_s, so_r.at[n], d_sib)

    def xo(n, d):
        return rc(x_out.at[n, d - 1], x_in.at[n, d - 1], xo_s, xo_r.at[n], d_x(d))

    def zo(n, d):
        return rc(t_out.at[n, d - 1], t_in.at[n, d - 1], zo_s.at[n], zo_r.at[n], d_z(d))

    def half(q, t=0, size=HALF):
        return pl.ds(pl.multiple_of(q * HALF + t * size, size), size)

    def st_z(b):
        @pl.when(mine(b))
        def _():
            for d in (1, 2, 3):
                zi(b, d).start()
            own_copy(b).start()

    def st_a(b):
        for h in range(2):
            @pl.when(zl != source(b, h))
            def _():
                arrived(xs.at[b, x, k, h], zi_r.at[b, h])

            @pl.when(zl == source(b, h))
            def _():
                own_copy(b).wait()
        for d in (1, 3, 2):
            xi(b, d).start()

    def st_c(b):
        arrived(xs.at[b, pl.ds(0, 3), k], xi_r.at[b])
        si(b).start()

    def st_d(n):
        b, q = n // 2, n % 2

        @pl.when(q == 0)
        def _():
            arrived(xs.at[b, :, 1 - k], si_r.at[b])

        @pl.when(n == 0)
        def _():
            w_cp.wait()

        acc = jnp.dot(xs[b].reshape(256, 1536), w[:, half(q)], preferred_element_type=F32)
        acc = acc.reshape(16, BLK, HALF)
        p32[n] = acc
        pb[n] = acc.astype(BF)

        for i in range(2):
            a_cp(n, i).start()
        for i in range(2):
            b_cp(n, i).start()

    def st_e(n):
        for i in range(2):
            arrived(a_in.at[n, i], a_r.at[n, i])
            r = gk((yp, ym)[i], i)
            pb[n, r] = (p32[n, r] + a_in[n, i].astype(F32)).astype(BF)
            c_cp(n, i).start()

    def st_f(n):
        arrived(bc_in.at[n], bc_r.at[n])
        for kk in range(2):
            def total(h):
                return (
                    p32[n, (y * 2 + kk) * 2 + h]
                    + bc_in[n, 0, kk, h].astype(F32)
                    + bc_in[n, 1, kk, h].astype(F32)
                )
            s_keep[n, kk] = total(zh)
            zs[n, kk] = total(1 - zh).astype(BF)
        zr(n).start()

    def st_g(n):
        b, q = n // 2, n % 2

        @pl.when(n == 0)
        def _():
            go_cp.wait()

        arrived(z_in.at[n], zr_r.at[n])
        line = part(b) * zh + (1 - part(b)) * (1 - zh)
        for kk in range(2):
            pre = s_keep[n, kk] + z_in[n, kk].astype(F32)
            cot = go[line, kk, b // 2, :, half(q)].astype(F32)
            gp[n, y, kk, zh] = (cot * gelu_slope(pre)).astype(BF)
        zg(n).start()

    def st_h(n):
        arrived(gp.at[n, y, :, 1 - zh], zg_r.at[n])
        for i in range(2):
            ga(n, i).start()
        for i in range(2):
            gb(n, i).start()

    def st_i(n):
        for i in range(2):
            arrived(gp.at[n, (ym, yp)[i], i], ga_r.at[n, i])
            gc(n, i).start()

    def st_j(n):
        b, q = n // 2, n % 2

        @pl.when(q == 0)
        def _():
            arrived(gp.at[pl.ds(2 * b, 2), pl.ds(0, 2)], gbc_r.at[b])

        @pl.loop(0, HALF // TILE)
        def _(t):
            rows = half(q, t, TILE)
            acc = 0.0
            for p in range(2):
                acc += lax.dot_general(
                    gp[2 * b + p].reshape(256, HALF),
                    w[rows, p * HALF : (p + 1) * HALF],
                    (((1,), (1,)), ((), ())),
                    preferred_element_type=F32,
                )
            g32[n, :, :, pl.ds(pl.multiple_of(t * TILE, TILE), TILE)] = acc.reshape(16, BLK, TILE)

        for g in range(4):
            sib_out[n, pl.ds(2 * g, 2)] = g32[n, gk(g, 1 - k)].astype(BF)
        so(n).start()

    def st_k(n):
        arrived(sib_in.at[n], so_r.at[n])

        def total(g):
            return g32[n, gk(g, k)] + sib_in[n, pl.ds(2 * g, 2)].astype(F32)

        for d in (1, 3, 2):
            x_out[n, d - 1] = total((x + d) % 4).astype(BF)
            xo(n, d).start()
        x_keep[n] = total(x)

    def st_l(n):
        b = n // 2
        arrived(x_in.at[n], xo_r.at[n])
        for h in range(2):
            tot = x_keep[n, h]
            for d in range(3):
                tot = tot + x_in[n, d, h].astype(F32)
            x_keep[n, h] = tot
            to = source(b, h)
            for d in (1, 2, 3):
                @pl.when((zl + d) % 4 == to)
                def _():
                    t_out[n, d - 1] = x_keep[n, h].astype(BF)
                    zo(n, d).start()

    def st_m(n):
        b, q = n // 2, n % 2

        @pl.when(mine(b))
        def _():
            tot = x_keep[n, zl // 2]
            arrived(t_in.at[n], zo_r.at[n])
            for d in range(3):
                tot = tot + t_in[n, d].astype(F32)
            out[b // 2, :, half(q)] = tot.astype(BF)

    def gw_out(t):
        rows = pl.ds(t * TILE if isinstance(t, int) else pl.multiple_of(t * TILE, TILE), TILE)
        return pltpu.make_async_copy(gwb.at[rows], gw_hbm.at[rows], gwsem.at[t])

    def gw_tile(t):
        o = pl.multiple_of(t * TILE, TILE)
        lhs = xs[:, :, :, :, :, pl.ds(o, TILE)].reshape(1024, TILE)
        for p in range(2):
            rhs = jnp.concatenate([gp[2 * b + p].reshape(256, HALF) for b in range(NB)], axis=0)
            acc = lax.dot_general(lhs, rhs, (((0,), (0,)), ((), ())), preferred_element_type=F32)
            gwb[pl.ds(o, TILE), p * HALF : (p + 1) * HALF] = acc.astype(BF)
        gw_out(t).start()

    stages = dict(z=st_z, a=st_a, c=st_c, d=st_d, e=st_e, f=st_f, g=st_g, h=st_h, i=st_i, j=st_j, k=st_k, l=st_l, m=st_m)

    @pl.loop(0, NSLOTS)
    def _(slot):
        for name, first in ORDER:
            n = slot - first
            go_now = (n >= 0) & (n < NS)
            if name in "zac":
                go_now = go_now & (n % 2 == 0)
                n = n // 2

            @pl.when(go_now)
            def _():
                stages[name](n)

        @pl.when((slot >= GW_FIRST) & (slot < GW_FIRST + 6 // GW_EACH))
        def _():
            @pl.loop(0, GW_EACH)
            def _(t):
                gw_tile((slot - GW_FIRST) * GW_EACH + t)

    for b in range(NB):
        @pl.when(mine(b))
        def _():
            sent(xs.at[b, pl.ds(0, 3), 0, 0], zi_s.at[b])

    for n in range(NS):
        @pl.when(mine(n // 2))
        def _():
            sent(t_out.at[n, 0], zo_s.at[n])

        @pl.when(jnp.logical_not(mine(n // 2)))
        def _():
            sent(t_out.at[n, pl.ds(0, 2)], zo_s.at[n])

    sent(xs.at[pl.ds(0, NB), pl.ds(0, 3), 0], xi_s)
    sent(xs.at[pl.ds(0, NB), :, 0], si_s)
    sent(pb.at[pl.ds(0, NS), pl.ds(0, 12)], abc_s)
    sent(zs, zr_s)
    sent(gp.at[pl.ds(0, NS), 0, 0], zg_s)
    sent(gp.at[pl.ds(0, NS), pl.ds(0, 3)], g_s)
    sent(sib_out, so_s)
    sent(x_out, xo_s)

    for t in range(6):
        gw_out(t).wait()


def place(gi, gw, gi_out, gw_out, gi_buf, gw_buf, in_sem, out_sem):
    size = 1536 // PIECES
    ways = []
    for p in range(PIECES):
        rows = pl.ds(p * size, size)
        ways.append((gw.at[rows], gw_buf.at[rows], gw_out.at[rows]))
    ways.append((gi, gi_buf, gi_out))
    into = [pltpu.make_async_copy(src, buf, in_sem.at[p]) for p, (src, buf, _) in enumerate(ways)]
    onto = [pltpu.make_async_copy(buf, dst, out_sem.at[p]) for p, (_, buf, dst) in enumerate(ways)]
    for copy in into:
        copy.start()
    for first, second in zip(into, onto):
        first.wait()
        second.start()
    for copy in onto:
        copy.wait()


def per_device(inputs, weight, grad_out):
    any_ = pl.BlockSpec(memory_space=pl.ANY)
    vmem = pl.BlockSpec(memory_space=pltpu.VMEM)
    V = pltpu.VMEM
    D = pltpu.SemaphoreType.DMA
    sems = [
        D((NB,)), D((NB, 2)),
        D, D((NB,)),
        D, D((NB,)),
        D, D((NS, 2)), D((NS,)),
        D, D((NS,)),
        D, D((NS,)),
        D, D((NS, 2)), D((NB,)),
        D, D((NS,)),
        D, D((NS,)),
        D((NS,)), D((NS,)),
    ]
    grad_inputs, grad_weight = pl.pallas_call(
        kernel,
        out_shape=(
            jax.ShapeDtypeStruct((2, BLK, 1536), BF),
            jax.ShapeDtypeStruct((1536, 1536), BF),
        ),
        in_specs=[vmem, any_, any_],
        out_specs=(vmem, any_),
        scratch_shapes=[
            V((1536, 1536), BF),
            V((2, 2, 2, BLK, 1536), BF),
            V((NB, 4, 2, 2, BLK, 1536), BF),
            V((NS, 16, BLK, HALF), F32),
            V((NS, 16, BLK, HALF), BF),
            V((NS, 2, 2, BLK, HALF), BF),
            V((NS, 2, 2, 2, BLK, HALF), BF),
            V((NS, 2, BLK, HALF), F32),
            V((NS, 2, BLK, HALF), BF),
            V((NS, 2, BLK, HALF), BF),
            V((NS, 4, 2, 2, BLK, HALF), BF),
            V((NS, 16, BLK, HALF), F32),
            V((NS, 8, BLK, HALF), BF),
            V((NS, 8, BLK, HALF), BF),
            V((NS, 3, 2, BLK, HALF), BF),
            V((NS, 3, 2, BLK, HALF), BF),
            V((NS, 2, BLK, HALF), F32),
            V((NS, 3, BLK, HALF), BF),
            V((NS, 3, BLK, HALF), BF),
            V((1536, 1536), BF),
            D((NB,)), D, D, D((6,)),
            *sems,
        ],
        compiler_params=pltpu.CompilerParams(
            collective_id=0, has_side_effects=True, vmem_limit_bytes=60 * 2**20
        ),
        cost_estimate=pl.CostEstimate(flops=3 * 2 * 1024 * 1536 * 1536, bytes_accessed=10**7, transcendentals=128 * 1536),
    )(inputs.reshape(2, BLK, 1536), weight, grad_out.reshape(2, 2, 2, BLK, 1536))
    grad_inputs, grad_weight = pl.pallas_call(
        place,
        out_shape=(jax.ShapeDtypeStruct((2, BLK, 1536), BF), jax.ShapeDtypeStruct((1536, 1536), BF)),
        in_specs=[any_, any_],
        out_specs=(any_, any_),
        scratch_shapes=[V((2, BLK, 1536), BF), V((1536, 1536), BF), D((PIECES + 1,)), D((PIECES + 1,))],
        compiler_params=pltpu.CompilerParams(vmem_limit_bytes=60 * 2**20),
    )(grad_inputs, grad_weight)
    return grad_inputs.reshape(32, 1536), grad_weight


def solution(mesh):
    return jax.shard_map(
        per_device,
        mesh=mesh,
        in_specs=(P("col", "row"), P("row", "col"), P("row", "col")),
        out_specs=(P("col", "row"), P("row", "col")),
        check_vma=False,
    )
```

```python
import math

import jax
import jax.numpy as jnp
from jax import lax
from jax.experimental import pallas as pl
from jax.experimental.pallas import tpu as pltpu
from jax.sharding import PartitionSpec as P

MESH = pl.DeviceIdType.MESH
NB = 4
BLK = 16
BF = jnp.bfloat16
F32 = jnp.float32
TILE = 256

PIECES = 8
HALF = 768
NS = 2 * NB

ORDER = (('h', 13), ('e', 8), ('l', 20), ('j', 16), ('g', 11), ('k', 17), ('m', 28), ('i', 14), ('f', 9), ('d', 6), ('a', 2), ('c', 5), ('z', 0))
NSLOTS = max(first for _, first in ORDER) + NS
GW_FIRST = dict(ORDER)["j"] + NS - 1
GW_EACH = 2


def gelu_slope(pre):
    coeff = math.sqrt(2.0 / math.pi)
    inner = coeff * (pre + 0.044715 * pre * pre * pre)
    tanh_val = jnp.tanh(inner)
    return 0.5 * (1.0 + tanh_val) + 0.5 * pre * (1.0 - tanh_val * tanh_val) * coeff * (
        1.0 + 3.0 * 0.044715 * pre * pre
    )


def kernel(
    inp, w_hbm, go_hbm,
    out, gw_hbm,
    w, go, xs, p32, pb, a_in, bc_in, s_keep, zs, z_in, gp, g32, sib_out, sib_in,
    x_out, x_in, x_keep, t_out, t_in, gwb,
    lsem, wsem, gsem, gwsem,
    zi_s, zi_r, xi_s, xi_r, si_s, si_r, abc_s, a_r, bc_r, zr_s, zr_r, zg_s, zg_r, g_s, ga_r, gbc_r,
    so_s, so_r, xo_s, xo_r, zo_s, zo_r,
):
    row = lax.axis_index("row")
    col = lax.axis_index("col")
    y, zh = row // 2, row % 2
    x, zl, k = col // 8, (col // 2) % 4, col % 2

    def dev(y=y, zh=zh, x=x, zl=zl, k=k):
        return (y * 2 + zh, (x * 4 + zl) * 2 + k)

    yp, ym = (y + 1) % 4, (y + 3) % 4
    yo = (y + 2) % 4
    d_yp, d_ym = dev(y=yp), dev(y=ym)
    d_zh = dev(zh=1 - zh)
    d_sib = dev(k=1 - k)

    def d_x(d):
        return dev(x=(x + d) % 4)

    def d_z(d):
        return dev(zl=(zl + d) % 4)

    def rc(src, dst, ss, rs, to):
        return pltpu.make_async_remote_copy(
            src_ref=src, dst_ref=dst, send_sem=ss, recv_sem=rs, device_id=to, device_id_type=MESH
        )

    w_cp = pltpu.make_async_copy(w_hbm, w, wsem)
    go_cp = pltpu.make_async_copy(go_hbm, go, gsem)
    w_cp.start()
    go_cp.start()

    barrier = pltpu.get_barrier_semaphore()
    partners = [d_yp, d_ym, d_zh, d_sib] + [d_x(d) for d in (1, 2, 3)] + [d_z(d) for d in (1, 2, 3)]
    for to in partners:
        pl.semaphore_signal(barrier, inc=1, device_id=to, device_id_type=MESH)
    pl.semaphore_wait(barrier, len(partners))

    def gk(g, kk):
        return pl.ds((g * 2 + kk) * 2, 2)

    def sent(region, sem):
        rc(region, region, sem, so_r.at[0], d_sib).wait_send()

    def arrived(region, sem):
        rc(region, region, so_s, sem, d_sib).wait_recv()

    def part(b):
        return ((b + 1) // 2) % 2

    def source(b, h):
        return (2 + part(b)) if h else (1 - part(b))

    def mine(b):
        return ((zl + 1) // 2) % 2 != part(b)

    def zi(b, d):
        return rc(inp.at[b // 2], xs.at[b, x, k, zl // 2], zi_s.at[b], zi_r.at[b, zl // 2], d_z(d))

    def own_copy(b):
        return pltpu.make_async_copy(inp.at[b // 2], xs.at[b, x, k, zl // 2], lsem.at[b])

    def xi(b, d):
        r = xs.at[b, x, k]
        return rc(r, r, xi_s, xi_r.at[b], d_x(d))

    def si(b):
        r = xs.at[b, :, k]
        return rc(r, r, si_s, si_r.at[b], d_sib)

    def a_cp(n, i):
        return rc(pb.at[n, gk(yo, i)], a_in.at[n, i], abc_s, a_r.at[n, i], (d_yp, d_ym)[i])

    def b_cp(n, i):
        return rc(pb.at[n, gk((yp, ym)[i], 1 - i)], bc_in.at[n, i, 1 - i], abc_s, bc_r.at[n], (d_yp, d_ym)[i])

    def c_cp(n, i):
        return rc(pb.at[n, gk((yp, ym)[i], i)], bc_in.at[n, i, i], abc_s, bc_r.at[n], (d_yp, d_ym)[i])

    def zr(n):
        return rc(zs.at[n], z_in.at[n], zr_s, zr_r.at[n], d_zh)

    def zg(n):
        r = gp.at[n, y, :, zh]
        return rc(r, r, zg_s, zg_r.at[n], d_zh)

    def ga(n, i):
        r = gp.at[n, y, i]
        return rc(r, r, g_s, ga_r.at[n, i], (d_yp, d_ym)[i])

    def gb(n, i):
        r = gp.at[n, y, 1 - i]
        return rc(r, r, g_s, gbc_r.at[n], (d_yp, d_ym)[i])

    def gc(n, i):
        r = gp.at[n, (ym, yp)[i], i]
        return rc(r, r, g_s, gbc_r.at[n], (d_yp, d_ym)[i])

    def so(n):
        return rc(sib_out.at[n], sib_in.at[n], so_s, so_r.at[n], d_sib)

    def xo(n, d):
        return rc(x_out.at[n, d - 1], x_in.at[n, d - 1], xo_s, xo_r.at[n], d_x(d))

    def zo(n, d):
        return rc(t_out.at[n, d - 1], t_in.at[n, d - 1], zo_s.at[n], zo_r.at[n], d_z(d))

    def half(q, t=0, size=HALF):
        return pl.ds(pl.multiple_of(q * HALF + t * size, size), size)

    def st_z(b):
        @pl.when(mine(b))
        def _():
            for d in (2, 1, 3):
                zi(b, d).start()
            own_copy(b).start()

    def st_a(b):
        for h in range(2):
            @pl.when(zl != source(b, h))
            def _():
                arrived(xs.at[b, x, k, h], zi_r.at[b, h])

            @pl.when(zl == source(b, h))
            def _():
                own_copy(b).wait()
        for d in (1, 3, 2):
            xi(b, d).start()

    def st_c(b):
        arrived(xs.at[b, pl.ds(0, 3), k], xi_r.at[b])
        si(b).start()

    def st_d(n):
        b, q = n // 2, n % 2

        @pl.when(q == 0)
        def _():
            arrived(xs.at[b, :, 1 - k], si_r.at[b])

        @pl.when(n == 0)
        def _():
            w_cp.wait()

        acc = jnp.dot(xs[b].reshape(256, 1536), w[:, half(q)], preferred_element_type=F32)
        acc = acc.reshape(16, BLK, HALF)
        p32[n] = acc
        pb[n] = acc.astype(BF)

        for i in range(2):
            a_cp(n, i).start()
        for i in range(2):
            b_cp(n, i).start()

    def st_e(n):
        for i in range(2):
            arrived(a_in.at[n, i], a_r.at[n, i])
            r = gk((yp, ym)[i], i)
            pb[n, r] = (p32[n, r] + a_in[n, i].astype(F32)).astype(BF)
            c_cp(n, i).start()

    def st_f(n):
        arrived(bc_in.at[n], bc_r.at[n])
        for kk in range(2):
            def total(h):
                return (
                    p32[n, (y * 2 + kk) * 2 + h]
                    + bc_in[n, 0, kk, h].astype(F32)
                    + bc_in[n, 1, kk, h].astype(F32)
                )
            s_keep[n, kk] = total(zh)
            zs[n, kk] = total(1 - zh).astype(BF)
        zr(n).start()

    def st_g(n):
        b, q = n // 2, n % 2

        @pl.when(n == 0)
        def _():
            go_cp.wait()

        arrived(z_in.at[n], zr_r.at[n])
        line = part(b) * zh + (1 - part(b)) * (1 - zh)
        for kk in range(2):
            pre = s_keep[n, kk] + z_in[n, kk].astype(F32)
            cot = go[line, kk, b // 2, :, half(q)].astype(F32)
            gp[n, y, kk, zh] = (cot * gelu_slope(pre)).astype(BF)
        zg(n).start()

    def st_h(n):
        arrived(gp.at[n, y, :, 1 - zh], zg_r.at[n])
        for i in range(2):
            ga(n, i).start()
        for i in range(2):
            gb(n, i).start()

    def st_i(n):
        for i in range(2):
            arrived(gp.at[n, (ym, yp)[i], i], ga_r.at[n, i])
            gc(n, i).start()

    def st_j(n):
        b, q = n // 2, n % 2
        arrived(gp.at[n, pl.ds(0, 2)], gbc_r.at[n])

        @pl.loop(0, 2)
        def _(r):
            m = 2 * b + r
            acc = lax.dot_general(
                gp[n].reshape(256, HALF), w[half(r), half(q)], (((1,), (1,)), ((), ())), preferred_element_type=F32
            ).reshape(16, BLK, HALF)

            @pl.when(q == 0)
            def _():
                g32[m] = acc

            @pl.when(q == 1)
            def _():
                g32[m] += acc
                for g in range(4):
                    sib_out[m, pl.ds(2 * g, 2)] = g32[m, gk(g, 1 - k)].astype(BF)
                so(m).start()

    def st_k(n):
        arrived(sib_in.at[n], so_r.at[n])

        def total(g):
            return g32[n, gk(g, k)] + sib_in[n, pl.ds(2 * g, 2)].astype(F32)

        for d in (1, 3, 2):
            x_out[n, d - 1] = total((x + d) % 4).astype(BF)
            xo(n, d).start()
        x_keep[n] = total(x)

    def st_l(n):
        b = n // 2
        arrived(x_in.at[n], xo_r.at[n])
        for h in range(2):
            tot = x_keep[n, h]
            for d in range(3):
                tot = tot + x_in[n, d, h].astype(F32)
            x_keep[n, h] = tot
            to = source(b, h)
            for d in (1, 2, 3):
                @pl.when((zl + d) % 4 == to)
                def _():
                    t_out[n, d - 1] = x_keep[n, h].astype(BF)
                    zo(n, d).start()

    def st_m(n):
        b, q = n // 2, n % 2

        @pl.when(mine(b))
        def _():
            tot = x_keep[n, zl // 2]
            arrived(t_in.at[n], zo_r.at[n])
            for d in range(3):
                tot = tot + t_in[n, d].astype(F32)
            out[b // 2, :, half(q)] = tot.astype(BF)

    def gw_out(t):
        rows = pl.ds(t * TILE if isinstance(t, int) else pl.multiple_of(t * TILE, TILE), TILE)
        return pltpu.make_async_copy(gwb.at[rows], gw_hbm.at[rows], gwsem.at[t])

    def gw_tile(t):
        o = pl.multiple_of(t * TILE, TILE)
        lhs = xs[:, :, :, :, :, pl.ds(o, TILE)].reshape(1024, TILE)
        for p in range(2):
            rhs = jnp.concatenate([gp[2 * b + p].reshape(256, HALF) for b in range(NB)], axis=0)
            acc = lax.dot_general(lhs, rhs, (((0,), (0,)), ((), ())), preferred_element_type=F32)
            gwb[pl.ds(o, TILE), p * HALF : (p + 1) * HALF] = acc.astype(BF)
        gw_out(t).start()

    stages = dict(z=st_z, a=st_a, c=st_c, d=st_d, e=st_e, f=st_f, g=st_g, h=st_h, i=st_i, j=st_j, k=st_k, l=st_l, m=st_m)

    @pl.loop(0, NSLOTS)
    def _(slot):
        for name, first in ORDER:
            n = slot - first
            go_now = (n >= 0) & (n < NS)
            if name in "zac":
                go_now = go_now & (n % 2 == 0)
                n = n // 2

            @pl.when(go_now)
            def _():
                stages[name](n)

        @pl.when((slot >= GW_FIRST) & (slot < GW_FIRST + 6 // GW_EACH))
        def _():
            @pl.loop(0, GW_EACH)
            def _(t):
                gw_tile((slot - GW_FIRST) * GW_EACH + t)

    for b in range(NB):
        @pl.when(mine(b))
        def _():
            sent(xs.at[b, pl.ds(0, 3), 0, 0], zi_s.at[b])

    for n in range(NS):
        @pl.when(mine(n // 2))
        def _():
            sent(t_out.at[n, 0], zo_s.at[n])

        @pl.when(jnp.logical_not(mine(n // 2)))
        def _():
            sent(t_out.at[n, pl.ds(0, 2)], zo_s.at[n])

    sent(xs.at[pl.ds(0, NB), pl.ds(0, 3), 0], xi_s)
    sent(xs.at[pl.ds(0, NB), :, 0], si_s)
    sent(pb.at[pl.ds(0, NS), pl.ds(0, 12)], abc_s)
    sent(zs, zr_s)
    sent(gp.at[pl.ds(0, NS), 0, 0], zg_s)
    sent(gp.at[pl.ds(0, NS), pl.ds(0, 3)], g_s)
    sent(sib_out, so_s)
    sent(x_out, xo_s)

    for t in range(6):
        gw_out(t).wait()


def place(gi, gw, gi_out, gw_out, gi_buf, gw_buf, in_sem, out_sem):
    size = 1536 // PIECES
    ways = []
    for p in range(PIECES):
        rows = pl.ds(p * size, size)
        ways.append((gw.at[rows], gw_buf.at[rows], gw_out.at[rows]))
    ways.append((gi, gi_buf, gi_out))
    into = [pltpu.make_async_copy(src, buf, in_sem.at[p]) for p, (src, buf, _) in enumerate(ways)]
    onto = [pltpu.make_async_copy(buf, dst, out_sem.at[p]) for p, (_, buf, dst) in enumerate(ways)]
    for copy in into:
        copy.start()
    for first, second in zip(into, onto):
        first.wait()
        second.start()
    for copy in onto:
        copy.wait()


def per_device(inputs, weight, grad_out):
    any_ = pl.BlockSpec(memory_space=pl.ANY)
    vmem = pl.BlockSpec(memory_space=pltpu.VMEM)
    V = pltpu.VMEM
    D = pltpu.SemaphoreType.DMA
    sems = [
        D((NB,)), D((NB, 2)),
        D, D((NB,)),
        D, D((NB,)),
        D, D((NS, 2)), D((NS,)),
        D, D((NS,)),
        D, D((NS,)),
        D, D((NS, 2)), D((NS,)),
        D, D((NS,)),
        D, D((NS,)),
        D((NS,)), D((NS,)),
    ]
    grad_inputs, grad_weight = pl.pallas_call(
        kernel,
        out_shape=(
            jax.ShapeDtypeStruct((2, BLK, 1536), BF),
            jax.ShapeDtypeStruct((1536, 1536), BF),
        ),
        in_specs=[vmem, any_, any_],
        out_specs=(vmem, any_),
        scratch_shapes=[
            V((1536, 1536), BF),
            V((2, 2, 2, BLK, 1536), BF),
            V((NB, 4, 2, 2, BLK, 1536), BF),
            V((NS, 16, BLK, HALF), F32),
            V((NS, 16, BLK, HALF), BF),
            V((NS, 2, 2, BLK, HALF), BF),
            V((NS, 2, 2, 2, BLK, HALF), BF),
            V((NS, 2, BLK, HALF), F32),
            V((NS, 2, BLK, HALF), BF),
            V((NS, 2, BLK, HALF), BF),
            V((NS, 4, 2, 2, BLK, HALF), BF),
            V((NS, 16, BLK, HALF), F32),
            V((NS, 8, BLK, HALF), BF),
            V((NS, 8, BLK, HALF), BF),
            V((NS, 3, 2, BLK, HALF), BF),
            V((NS, 3, 2, BLK, HALF), BF),
            V((NS, 2, BLK, HALF), F32),
            V((NS, 3, BLK, HALF), BF),
            V((NS, 3, BLK, HALF), BF),
            V((1536, 1536), BF),
            D((NB,)), D, D, D((6,)),
            *sems,
        ],
        compiler_params=pltpu.CompilerParams(
            collective_id=0, has_side_effects=True, vmem_limit_bytes=60 * 2**20
        ),
        cost_estimate=pl.CostEstimate(flops=3 * 2 * 1024 * 1536 * 1536, bytes_accessed=10**7, transcendentals=128 * 1536),
    )(inputs.reshape(2, BLK, 1536), weight, grad_out.reshape(2, 2, 2, BLK, 1536))
    grad_inputs, grad_weight = pl.pallas_call(
        place,
        out_shape=(jax.ShapeDtypeStruct((2, BLK, 1536), BF), jax.ShapeDtypeStruct((1536, 1536), BF)),
        in_specs=[any_, any_],
        out_specs=(any_, any_),
        scratch_shapes=[V((2, BLK, 1536), BF), V((1536, 1536), BF), D((PIECES + 1,)), D((PIECES + 1,))],
        compiler_params=pltpu.CompilerParams(vmem_limit_bytes=60 * 2**20),
    )(grad_inputs, grad_weight)
    return grad_inputs.reshape(32, 1536), grad_weight


def solution(mesh):
    return jax.shard_map(
        per_device,
        mesh=mesh,
        in_specs=(P("col", "row"), P("row", "col"), P("row", "col")),
        out_specs=(P("col", "row"), P("row", "col")),
        check_vma=False,
    )
```

```python
import math

import jax
import jax.numpy as jnp
from jax import lax
from jax.experimental import pallas as pl
from jax.experimental.pallas import tpu as pltpu
from jax.sharding import PartitionSpec as P

MESH = pl.DeviceIdType.MESH
NB = 4
BLK = 16
BF = jnp.bfloat16
F32 = jnp.float32
TILE = 256

PIECES = 8
HALF = 768
NS = 2 * NB

ORDER = (('h', 13), ('e', 8), ('l', 20), ('j', 16), ('g', 11), ('k', 17), ('m', 28), ('i', 14), ('f', 9), ('d', 6), ('a', 2), ('c', 5), ('z', 0))
NSLOTS = max(first for _, first in ORDER) + NS
GW_FIRST = dict(ORDER)["j"] + NS
GW_EACH = 2


def gelu_slope(pre):
    coeff = math.sqrt(2.0 / math.pi)
    inner = coeff * (pre + 0.044715 * pre * pre * pre)
    tanh_val = jnp.tanh(inner)
    return 0.5 * (1.0 + tanh_val) + 0.5 * pre * (1.0 - tanh_val * tanh_val) * coeff * (
        1.0 + 3.0 * 0.044715 * pre * pre
    )


def kernel(
    inp, w_hbm, go_hbm,
    out, gw_hbm,
    w, go, xs, p32, pb, a_in, bc_in, s_keep, zs, z_in, gp, g32, sib_out, sib_in,
    x_out, x_in, x_keep, t_out, t_in, gwb,
    lsem, wsem, gsem, gwsem,
    zi_s, zi_r, xi_s, xi_r, si_s, si_r, abc_s, a_r, bc_r, zr_s, zr_r, zg_s, zg_r, g_s, ga_r, gbc_r,
    so_s, so_r, xo_s, xo_r, zo_s, zo_r,
):
    row = lax.axis_index("row")
    col = lax.axis_index("col")
    y, zh = row // 2, row % 2
    x, zl, k = col // 8, (col // 2) % 4, col % 2

    def dev(y=y, zh=zh, x=x, zl=zl, k=k):
        return (y * 2 + zh, (x * 4 + zl) * 2 + k)

    yp, ym = (y + 1) % 4, (y + 3) % 4
    yo = (y + 2) % 4
    d_yp, d_ym = dev(y=yp), dev(y=ym)
    d_zh = dev(zh=1 - zh)
    d_sib = dev(k=1 - k)

    def d_x(d):
        return dev(x=(x + d) % 4)

    def d_z(d):
        return dev(zl=(zl + d) % 4)

    def rc(src, dst, ss, rs, to):
        return pltpu.make_async_remote_copy(
            src_ref=src, dst_ref=dst, send_sem=ss, recv_sem=rs, device_id=to, device_id_type=MESH
        )

    w_cp = pltpu.make_async_copy(w_hbm, w, wsem)
    go_cp = pltpu.make_async_copy(go_hbm, go, gsem)
    w_cp.start()
    go_cp.start()

    barrier = pltpu.get_barrier_semaphore()
    partners = [d_yp, d_ym, d_zh, d_sib] + [d_x(d) for d in (1, 2, 3)] + [d_z(d) for d in (1, 2, 3)]
    for to in partners:
        pl.semaphore_signal(barrier, inc=1, device_id=to, device_id_type=MESH)
    pl.semaphore_wait(barrier, len(partners))

    def gk(g, kk):
        return pl.ds((g * 2 + kk) * 2, 2)

    def sent(region, sem):
        rc(region, region, sem, so_r.at[0], d_sib).wait_send()

    def arrived(region, sem):
        rc(region, region, so_s, sem, d_sib).wait_recv()

    def part(b):
        return ((b + 1) // 2) % 2

    def source(b, h):
        return (2 + part(b)) if h else (1 - part(b))

    def mine(b):
        return ((zl + 1) // 2) % 2 != part(b)

    def zi(b, d):
        return rc(inp.at[b // 2], xs.at[b, x, k, zl // 2], zi_s.at[b], zi_r.at[b, zl // 2], d_z(d))

    def own_copy(b):
        return pltpu.make_async_copy(inp.at[b // 2], xs.at[b, x, k, zl // 2], lsem.at[b])

    def xi(b, d):
        r = xs.at[b, x, k]
        return rc(r, r, xi_s, xi_r.at[b], d_x(d))

    def si(b):
        r = xs.at[b, :, k]
        return rc(r, r, si_s, si_r.at[b], d_sib)

    def a_cp(n, i):
        return rc(pb.at[n, gk(yo, i)], a_in.at[n, i], abc_s, a_r.at[n, i], (d_yp, d_ym)[i])

    def b_cp(n, i):
        return rc(pb.at[n, gk((yp, ym)[i], 1 - i)], bc_in.at[n, i, 1 - i], abc_s, bc_r.at[n], (d_yp, d_ym)[i])

    def c_cp(n, i):
        return rc(pb.at[n, gk((yp, ym)[i], i)], bc_in.at[n, i, i], abc_s, bc_r.at[n], (d_yp, d_ym)[i])

    def zr(n):
        return rc(zs.at[n], z_in.at[n], zr_s, zr_r.at[n], d_zh)

    def zg(n):
        r = gp.at[n, y, :, zh]
        return rc(r, r, zg_s, zg_r.at[n], d_zh)

    def ga(n, i):
        r = gp.at[n, y, i]
        return rc(r, r, g_s, ga_r.at[n, i], (d_yp, d_ym)[i])

    def gb(n, i):
        r = gp.at[n, y, 1 - i]
        return rc(r, r, g_s, gbc_r.at[n], (d_yp, d_ym)[i])

    def gc(n, i):
        r = gp.at[n, (ym, yp)[i], i]
        return rc(r, r, g_s, gbc_r.at[n], (d_yp, d_ym)[i])

    def so(n):
        return rc(sib_out.at[n], sib_in.at[n], so_s, so_r.at[n], d_sib)

    def xo(n, d):
        return rc(x_out.at[n, d - 1], x_in.at[n, d - 1], xo_s, xo_r.at[n], d_x(d))

    def zo(n, d):
        return rc(t_out.at[n, d - 1], t_in.at[n, d - 1], zo_s.at[n], zo_r.at[n], d_z(d))

    def half(q, t=0, size=HALF):
        return pl.ds(pl.multiple_of(q * HALF + t * size, size), size)

    def st_z(b):
        @pl.when(mine(b))
        def _():
            for d in (2, 1, 3):
                zi(b, d).start()
            own_copy(b).start()

    def st_a(b):
        for h in range(2):
            @pl.when(zl != source(b, h))
            def _():
                arrived(xs.at[b, x, k, h], zi_r.at[b, h])

            @pl.when(zl == source(b, h))
            def _():
                own_copy(b).wait()
        for d in (1, 3, 2):
            xi(b, d).start()

    def st_c(b):
        arrived(xs.at[b, pl.ds(0, 3), k], xi_r.at[b])
        si(b).start()

    def st_d(n):
        b, q = n // 2, n % 2

        @pl.when(q == 0)
        def _():
            arrived(xs.at[b, :, 1 - k], si_r.at[b])

        @pl.when(n == 0)
        def _():
            w_cp.wait()

        acc = jnp.dot(xs[b].reshape(256, 1536), w[:, half(q)], preferred_element_type=F32)
        acc = acc.reshape(16, BLK, HALF)
        p32[n] = acc
        pb[n] = acc.astype(BF)

        for i in range(2):
            a_cp(n, i).start()
        for i in range(2):
            b_cp(n, i).start()

    def st_e(n):
        for i in range(2):
            arrived(a_in.at[n, i], a_r.at[n, i])
            r = gk((yp, ym)[i], i)
            pb[n, r] = (p32[n, r] + a_in[n, i].astype(F32)).astype(BF)
            c_cp(n, i).start()

    def st_f(n):
        arrived(bc_in.at[n], bc_r.at[n])
        for kk in range(2):
            def total(h):
                return (
                    p32[n, (y * 2 + kk) * 2 + h]
                    + bc_in[n, 0, kk, h].astype(F32)
                    + bc_in[n, 1, kk, h].astype(F32)
                )
            s_keep[n, kk] = total(zh)
            zs[n, kk] = total(1 - zh).astype(BF)
        zr(n).start()

    def st_g(n):
        b, q = n // 2, n % 2

        @pl.when(n == 0)
        def _():
            go_cp.wait()

        arrived(z_in.at[n], zr_r.at[n])
        line = part(b) * zh + (1 - part(b)) * (1 - zh)
        for kk in range(2):
            pre = s_keep[n, kk] + z_in[n, kk].astype(F32)
            cot = go[line, kk, b // 2, :, half(q)].astype(F32)
            gp[n, y, kk, zh] = (cot * gelu_slope(pre)).astype(BF)
        zg(n).start()

    def st_h(n):
        arrived(gp.at[n, y, :, 1 - zh], zg_r.at[n])
        for i in range(2):
            ga(n, i).start()
        for i in range(2):
            gb(n, i).start()

    def st_i(n):
        for i in range(2):
            arrived(gp.at[n, (ym, yp)[i], i], ga_r.at[n, i])
            gc(n, i).start()

    def st_j(n):
        b, q = n // 2, n % 2
        arrived(gp.at[n, pl.ds(0, 2)], gbc_r.at[n])

        @pl.loop(0, 2)
        def _(r):
            m = 2 * b + r
            acc = lax.dot_general(
                gp[n].reshape(256, HALF), w[half(r), half(q)], (((1,), (1,)), ((), ())), preferred_element_type=F32
            ).reshape(16, BLK, HALF)

            @pl.when(q == 0)
            def _():
                g32[m] = acc

            @pl.when(q == 1)
            def _():
                g32[m] += acc
                for g in range(4):
                    sib_out[m, pl.ds(2 * g, 2)] = g32[m, gk(g, 1 - k)].astype(BF)
                so(m).start()

    def st_k(n):
        arrived(sib_in.at[n], so_r.at[n])

        def total(g):
            return g32[n, gk(g, k)] + sib_in[n, pl.ds(2 * g, 2)].astype(F32)

        for d in (1, 3, 2):
            x_out[n, d - 1] = total((x + d) % 4).astype(BF)
            xo(n, d).start()
        x_keep[n] = total(x)

    def st_l(n):
        b = n // 2
        arrived(x_in.at[n], xo_r.at[n])
        for h in range(2):
            tot = x_keep[n, h]
            for d in range(3):
                tot = tot + x_in[n, d, h].astype(F32)
            x_keep[n, h] = tot
            to = source(b, h)
            for d in (1, 2, 3):
                @pl.when((zl + d) % 4 == to)
                def _():
                    t_out[n, d - 1] = x_keep[n, h].astype(BF)
                    zo(n, d).start()

    def st_m(n):
        b, q = n // 2, n % 2

        @pl.when(mine(b))
        def _():
            tot = x_keep[n, zl // 2]
            arrived(t_in.at[n], zo_r.at[n])
            for d in range(3):
                tot = tot + t_in[n, d].astype(F32)
            out[b // 2, :, half(q)] = tot.astype(BF)

    def gw_out(t):
        rows = pl.ds(t * TILE if isinstance(t, int) else pl.multiple_of(t * TILE, TILE), TILE)
        return pltpu.make_async_copy(gwb.at[rows], gw_hbm.at[rows], gwsem.at[t])

    def gw_tile(t):
        o = pl.multiple_of(t * TILE, TILE)
        lhs = xs[:, :, :, :, :, pl.ds(o, TILE)].reshape(1024, TILE)
        for p in range(2):
            rhs = jnp.concatenate([gp[2 * b + p].reshape(256, HALF) for b in range(NB)], axis=0)
            acc = lax.dot_general(lhs, rhs, (((0,), (0,)), ((), ())), preferred_element_type=F32)
            gwb[pl.ds(o, TILE), p * HALF : (p + 1) * HALF] = acc.astype(BF)
        gw_out(t).start()

    stages = dict(z=st_z, a=st_a, c=st_c, d=st_d, e=st_e, f=st_f, g=st_g, h=st_h, i=st_i, j=st_j, k=st_k, l=st_l, m=st_m)

    @pl.loop(0, NSLOTS)
    def _(slot):
        for name, first in ORDER:
            n = slot - first
            go_now = (n >= 0) & (n < NS)
            if name in "zac":
                go_now = go_now & (n % 2 == 0)
                n = n // 2

            @pl.when(go_now)
            def _():
                stages[name](n)

        @pl.when((slot >= GW_FIRST) & (slot < GW_FIRST + 6 // GW_EACH))
        def _():
            @pl.loop(0, GW_EACH)
            def _(t):
                gw_tile((slot - GW_FIRST) * GW_EACH + t)

    for b in range(NB):
        @pl.when(mine(b))
        def _():
            sent(xs.at[b, pl.ds(0, 3), 0, 0], zi_s.at[b])

    for n in range(NS):
        @pl.when(mine(n // 2))
        def _():
            sent(t_out.at[n, 0], zo_s.at[n])

        @pl.when(jnp.logical_not(mine(n // 2)))
        def _():
            sent(t_out.at[n, pl.ds(0, 2)], zo_s.at[n])

    sent(xs.at[pl.ds(0, NB), pl.ds(0, 3), 0], xi_s)
    sent(xs.at[pl.ds(0, NB), :, 0], si_s)
    sent(pb.at[pl.ds(0, NS), pl.ds(0, 12)], abc_s)
    sent(zs, zr_s)
    sent(gp.at[pl.ds(0, NS), 0, 0], zg_s)
    sent(gp.at[pl.ds(0, NS), pl.ds(0, 3)], g_s)
    sent(sib_out, so_s)
    sent(x_out, xo_s)

    for t in range(6):
        gw_out(t).wait()


def place(gi, gw, gi_out, gw_out, gi_buf, gw_buf, in_sem, out_sem):
    size = 1536 // PIECES
    ways = []
    for p in range(PIECES):
        rows = pl.ds(p * size, size)
        ways.append((gw.at[rows], gw_buf.at[rows], gw_out.at[rows]))
    ways.append((gi, gi_buf, gi_out))
    into = [pltpu.make_async_copy(src, buf, in_sem.at[p]) for p, (src, buf, _) in enumerate(ways)]
    onto = [pltpu.make_async_copy(buf, dst, out_sem.at[p]) for p, (_, buf, dst) in enumerate(ways)]
    for copy in into:
        copy.start()
    for first, second in zip(into, onto):
        first.wait()
        second.start()
    for copy in onto:
        copy.wait()


def per_device(inputs, weight, grad_out):
    any_ = pl.BlockSpec(memory_space=pl.ANY)
    vmem = pl.BlockSpec(memory_space=pltpu.VMEM)
    V = pltpu.VMEM
    D = pltpu.SemaphoreType.DMA
    sems = [
        D((NB,)), D((NB, 2)),
        D, D((NB,)),
        D, D((NB,)),
        D, D((NS, 2)), D((NS,)),
        D, D((NS,)),
        D, D((NS,)),
        D, D((NS, 2)), D((NS,)),
        D, D((NS,)),
        D, D((NS,)),
        D((NS,)), D((NS,)),
    ]
    grad_inputs, grad_weight = pl.pallas_call(
        kernel,
        out_shape=(
            jax.ShapeDtypeStruct((2, BLK, 1536), BF),
            jax.ShapeDtypeStruct((1536, 1536), BF),
        ),
        in_specs=[vmem, any_, any_],
        out_specs=(vmem, any_),
        scratch_shapes=[
            V((1536, 1536), BF),
            V((2, 2, 2, BLK, 1536), BF),
            V((NB, 4, 2, 2, BLK, 1536), BF),
            V((NS, 16, BLK, HALF), F32),
            V((NS, 16, BLK, HALF), BF),
            V((NS, 2, 2, BLK, HALF), BF),
            V((NS, 2, 2, 2, BLK, HALF), BF),
            V((NS, 2, BLK, HALF), F32),
            V((NS, 2, BLK, HALF), BF),
            V((NS, 2, BLK, HALF), BF),
            V((NS, 4, 2, 2, BLK, HALF), BF),
            V((NS, 16, BLK, HALF), F32),
            V((NS, 8, BLK, HALF), BF),
            V((NS, 8, BLK, HALF), BF),
            V((NS, 3, 2, BLK, HALF), BF),
            V((NS, 3, 2, BLK, HALF), BF),
            V((NS, 2, BLK, HALF), F32),
            V((NS, 3, BLK, HALF), BF),
            V((NS, 3, BLK, HALF), BF),
            V((1536, 1536), BF),
            D((NB,)), D, D, D((6,)),
            *sems,
        ],
        compiler_params=pltpu.CompilerParams(
            collective_id=0, has_side_effects=True, vmem_limit_bytes=60 * 2**20
        ),
        cost_estimate=pl.CostEstimate(flops=3 * 2 * 1024 * 1536 * 1536, bytes_accessed=10**7, transcendentals=128 * 1536),
    )(inputs.reshape(2, BLK, 1536), weight, grad_out.reshape(2, 2, 2, BLK, 1536))
    grad_inputs, grad_weight = pl.pallas_call(
        place,
        out_shape=(jax.ShapeDtypeStruct((2, BLK, 1536), BF), jax.ShapeDtypeStruct((1536, 1536), BF)),
        in_specs=[any_, any_],
        out_specs=(any_, any_),
        scratch_shapes=[V((2, BLK, 1536), BF), V((1536, 1536), BF), D((PIECES + 1,)), D((PIECES + 1,))],
        compiler_params=pltpu.CompilerParams(vmem_limit_bytes=60 * 2**20),
    )(grad_inputs, grad_weight)
    return grad_inputs.reshape(32, 1536), grad_weight


def solution(mesh):
    return jax.shard_map(
        per_device,
        mesh=mesh,
        in_specs=(P("col", "row"), P("row", "col"), P("row", "col")),
        out_specs=(P("col", "row"), P("row", "col")),
        check_vma=False,
    )
```
